32 devices in a mesh: seq: 4 (over y, x), mp: 8 (over z, core).
Axes of the slice: x: 2, y: 2, z: 4, core: 2. Of those that a mesh axis runs over, the one named last changes fastest.
Arguments:
- features: bfloat16 [8192, 16384], P('seq', 'mp'), may hold values from -6 to 6
- coupling: bfloat16 [8192, 256], P('seq'), may hold values from -6 to 6
- gate_values: bfloat16 [8192, 16384], P('seq', 'mp'), may hold values from -40 to 40
- step_raw: float32 [256, 8192], P('mp', 'seq'), may hold values from -12 to 8192
- decay_log: float32 [256], P('mp'), may hold values from -8 to 0
- feature_taps: float32 [4, 16384], P(None, 'mp'), may hold values from -3 to 3
- feature_offset: float32 [16384], P('mp'), may hold values from -3 to 3
- coupling_taps: float32 [4, 256], replicated, may hold values from -3 to 3
- coupling_offset: float32 [256], replicated, may hold values from -3 to 3
- norm_gain: float32 [16384], P('mp'), may hold values from 0.25 to 1.75
Outputs:
- normalized: bfloat16 [8192, 16384], P('seq', 'mp')
The draws below stay inside these ranges and needn't reach their ends.
All inputs are finite; a program needn't handle non-finite values.
Results may differ from the reference program's by a relative error of at most 0.0061.
Values may be sent and summed in bfloat16 or wider, within the bound.
A program may use at most 128 MiB of HBM per device.

```python
import math
import jax
import jax.numpy as jnp
from jax import lax

TOK_DEV = 2048
HEAD_TOTAL = 256
HEAD_DIM = 64
STATE = 128
KCONV = 4
BLOCK = 256
SEQUENCE_TOKENS = 8192
INNER = 16384


def decay_plan(key):
    random_key_series = jax.random.split(jax.random.fold_in(key, 101), 7)
    fast_share = 0.5
    is_fast = jax.random.uniform(random_key_series[0], (HEAD_TOTAL,)) < fast_share
    rate_fast = jnp.exp(jax.random.uniform(random_key_series[1], (HEAD_TOTAL,), minval=math.log(1.0 / 50.0), maxval=math.log(1.0 / 30.0)))
    rate_slow = jnp.exp(jax.random.uniform(random_key_series[2], (HEAD_TOTAL,), minval=math.log(0.2), maxval=math.log(0.8))) / SEQUENCE_TOKENS
    rate_value = jnp.where(is_fast, rate_fast, rate_slow)
    typical = 0.5 * jnp.sqrt(jnp.maximum(rate_value, 1.0 / SEQUENCE_TOKENS))
    spike_amplitude = rate_value / typical
    sections = SEQUENCE_TOKENS // TOK_DEV
    section_factor = jnp.exp(jax.random.uniform(random_key_series[3], (sections, HEAD_TOTAL), minval=math.log(0.5), maxval=math.log(1.5)))
    section_factor = jnp.repeat(section_factor, TOK_DEV, axis=0, total_repeat_length=SEQUENCE_TOKENS)
    jitter = jnp.exp(jax.random.uniform(random_key_series[4], (SEQUENCE_TOKENS, HEAD_TOTAL), minval=math.log(0.7), maxval=math.log(1.4)))
    increment_amount = typical[None, :] * section_factor * jitter
    spike_locations = jax.random.randint(random_key_series[5], (2,), 0, SEQUENCE_TOKENS)
    spike_penalty = jax.random.uniform(random_key_series[6], (2, HEAD_TOTAL), minval=0.2, maxval=0.35)
    spike_increment = -jnp.log1p(-spike_penalty) / spike_amplitude[None, :]
    token_locations = jnp.arange(SEQUENCE_TOKENS)
    earliest_match = (token_locations == spike_locations[0])[:, None]
    latter_match = (token_locations == spike_locations[1])[:, None]
    complete_increment = jnp.where(earliest_match, spike_increment[0][None, :], increment_amount)
    complete_increment = jnp.where(latter_match, spike_increment[1][None, :], complete_increment)
    damping = jnp.minimum(1.0, increment_amount / complete_increment)
    return (spike_amplitude, complete_increment, damping)


def draw_features(key, part):
    spike_amplitude, complete_increment, damping = decay_plan(key)
    noise_key = jax.random.fold_in(key, 202)
    noise_field = jax.random.normal(noise_key, (SEQUENCE_TOKENS, HEAD_TOTAL, HEAD_DIM))
    values = jnp.clip(noise_field * damping[:, :, None], -6.0, 6.0)
    return values.reshape(SEQUENCE_TOKENS, INNER).astype(jnp.bfloat16)


def draw_step_raw(key, part):
    spike_amplitude, complete_increment, damping = decay_plan(key)
    raw_values = complete_increment + jnp.log1p(-jnp.exp(-complete_increment))
    return raw_values.T.astype(jnp.float32)


def draw_decay_log(key, part):
    spike_amplitude, complete_increment, damping = decay_plan(key)
    return jnp.log(spike_amplitude).astype(jnp.float32)


def draw_gate_values(key, part):
    random_key_series = jax.random.split(jax.random.fold_in(key, 303), 3)
    columns = jnp.arange(INNER).astype(jnp.float32) / INNER
    row_scale = jnp.exp(jax.random.uniform(random_key_series[0], (SEQUENCE_TOKENS, 1), minval=math.log(0.5), maxval=math.log(5.0)))
    col_scale = 0.3 * jnp.power(10.0, columns)
    noise_field = jax.random.normal(random_key_series[2], (SEQUENCE_TOKENS, INNER))
    values = jnp.clip(noise_field * col_scale[None, :] * row_scale, -40.0, 40.0)
    return values.astype(jnp.bfloat16)


def block_levels(own_key, extent, shards, low, top_value):
    level = 1.0
    for axis_at, shards_of in shards:
        steps = jax.random.uniform(jax.random.fold_in(jax.random.fold_in(own_key, 6), axis_at), (shards_of,), jnp.float32, low / len(shards), top_value / len(shards))
        level = level * jnp.repeat(jnp.exp(steps), extent[axis_at] // shards_of).reshape((-1,) + (1,) * (len(extent) - 1 - axis_at))
    return level


def normal_values(own_key, shape, scale, most, cuts=(), held_as=jnp.bfloat16):
    entries = scale * jax.random.normal(own_key, shape, jnp.float32)
    if cuts:
        entries = entries * block_levels(own_key, shape, cuts, -0.22, 0.18)
    return jnp.clip(entries, -most, most).astype(held_as)


def setup_inputs(seed: int = 0) -> dict:
    streams_of = jax.random.split(jax.random.key(seed), 11)
    features = draw_features(jax.random.fold_in(streams_of[10], 71), 0)
    coupling = normal_values(streams_of[1], (SEQUENCE_TOKENS, 2 * STATE), 1.0, 6.0, ((0, 4),))
    gate_values = draw_gate_values(jax.random.fold_in(streams_of[10], 71), 0)
    step_raw = draw_step_raw(jax.random.fold_in(streams_of[10], 71), 0)
    decay_log = draw_decay_log(jax.random.fold_in(streams_of[10], 71), 0)
    feature_taps = normal_values(streams_of[5], (KCONV, INNER), KCONV ** -0.5, 3.0, ((1, 8),), jnp.float32)
    feature_offset = normal_values(streams_of[6], (INNER,), 0.5, 3.0, ((0, 8),), jnp.float32)
    coupling_taps = normal_values(streams_of[7], (KCONV, 2 * STATE), KCONV ** -0.5, 3.0, (), jnp.float32)
    coupling_offset = normal_values(streams_of[8], (2 * STATE,), 0.5, 3.0, (), jnp.float32)
    norm_gain = jnp.clip(1.0 + 0.15 * jax.random.normal(streams_of[9], (INNER,), jnp.float32), 0.25, 1.75)
    return {"features": features, "coupling": coupling, "gate_values": gate_values, "step_raw": step_raw, "decay_log": decay_log, "feature_taps": feature_taps, "feature_offset": feature_offset, "coupling_taps": coupling_taps, "coupling_offset": coupling_offset, "norm_gain": norm_gain}


FULL_PRECISION = lax.Precision.HIGHEST

def causal_mix(previous, current, weight, bias_row):
    tap_count = weight.shape[0]
    length = current.shape[0]
    padded = jnp.concatenate([previous, current], axis=0)
    running = jnp.zeros(current.shape, jnp.float32) + bias_row[None, :]
    for offset in range(tap_count):
        running = running + weight[offset][None, :] * padded[offset:offset + length].astype(jnp.float32)
    return jax.nn.silu(running).astype(jnp.bfloat16)

def block_pass(state_now, feature_block, input_map, output_map, step_block, log_block):
    head_count, block_len = step_block.shape
    feature = feature_block.shape[1] // head_count
    per_head = feature_block.astype(jnp.float32).reshape(block_len, head_count, feature)
    scores = jnp.dot(output_map, input_map.T, precision=FULL_PRECISION)
    spread = log_block[:, :, None] - log_block[:, None, :]
    causal = (jnp.arange(block_len)[:, None] >= jnp.arange(block_len)[None, :])[None, :, :]
    weights = jnp.where(causal, jnp.exp(jnp.where(causal, spread, 0.0)), 0.0)
    weights = weights * scores[None, :, :] * step_block[:, None, :]
    inside = jnp.einsum('hts,shp->thp', weights, per_head, precision=FULL_PRECISION)
    carried = jnp.einsum('tn,hpn->thp', output_map, state_now, precision=FULL_PRECISION)
    carried = carried * jnp.exp(log_block).T[:, :, None]
    ending = log_block[:, -1]
    to_end = jnp.exp(ending[:, None] - log_block) * step_block
    weighted = per_head * to_end.T[:, :, None]
    fresh_part = jnp.einsum('shp,sn->hpn', weighted, input_map, precision=FULL_PRECISION)
    new_state = jnp.exp(ending)[:, None, None] * state_now + fresh_part
    return (new_state, (inside + carried).reshape(block_len, head_count * feature))

def reference(features, coupling, gate_values, step_raw, decay_log, feature_taps, feature_offset, coupling_taps, coupling_offset, norm_gain):
    tap_count = feature_taps.shape[0]
    head_count = decay_log.shape[0]
    state_size = coupling.shape[1] // 2
    feature = features.shape[1] // head_count
    blocks = SEQUENCE_TOKENS // BLOCK
    rate_values = jnp.exp(decay_log)

    def advance(carried_in, inputs):
        state_now, prior_features, prior_coupling = carried_in
        feature_block, coupling_block, gate_block, raw_block = inputs
        filtered = causal_mix(prior_features, feature_block, feature_taps, feature_offset)
        coupled = causal_mix(prior_coupling, coupling_block, coupling_taps, coupling_offset).astype(jnp.float32)
        step_block = jax.nn.softplus(raw_block)
        log_block = jnp.cumsum(-rate_values[:, None] * step_block, axis=1)
        new_state, output = block_pass(state_now, filtered, coupled[:, :state_size], coupled[:, state_size:], step_block, log_block)
        gated_values = output * jax.nn.silu(gate_block.astype(jnp.float32))
        mean_square = lax.optimization_barrier(jnp.mean(gated_values * gated_values, axis=1))
        result = (gated_values * norm_gain[None, :] * lax.rsqrt(mean_square + 1e-05)[:, None]).astype(jnp.bfloat16)
        tail_rows = tap_count - 1
        return ((new_state, feature_block[BLOCK - tail_rows:], coupling_block[BLOCK - tail_rows:]), result)
    zero_state = jnp.zeros((head_count, feature, state_size), jnp.float32)
    prior_features = jnp.zeros((tap_count - 1, features.shape[1]), jnp.bfloat16)
    prior_coupling = jnp.zeros((tap_count - 1, coupling.shape[1]), jnp.bfloat16)
    inputs = (features.reshape(blocks, BLOCK, features.shape[1]), coupling.reshape(blocks, BLOCK, coupling.shape[1]), gate_values.reshape(blocks, BLOCK, gate_values.shape[1]), step_raw.reshape(head_count, blocks, BLOCK).transpose(1, 0, 2))
    final_carry, results = lax.scan(advance, (zero_state, prior_features, prior_coupling), inputs)
    return results.reshape(SEQUENCE_TOKENS, features.shape[1])
```

```python
import functools
import jax
import jax.numpy as jnp
from jax import lax
from jax.sharding import PartitionSpec as P
from jax.experimental import pallas as pl
from jax.experimental.pallas import tpu as pltpu

INNER = 16384
Q = 128
STATE = 128
HEAD = 64
LOG2E = 1.4426950408889634
F32 = jnp.float32
BF = jnp.bfloat16
HI = lax.Precision.HIGHEST
VMEM_LIMIT = 48 * 1024 * 1024


def iota(shape, dim):
    return lax.broadcasted_iota(jnp.int32, shape, dim)


def dot(a, b, **kw):
    return jnp.dot(a, b, preferred_element_type=F32, **kw)


def dot_rows(a, b, **kw):
    return lax.dot_general(a, b, (((1,), (1,)), ((), ())), preferred_element_type=F32, **kw)


def silu(v):
    return v * pl.reciprocal(1.0 + jnp.exp2(v * -LOG2E), approx=True)


def split3(v):
    hi = v.astype(BF).astype(F32)
    mid = (v - hi).astype(BF).astype(F32)
    return hi, mid, (v - hi) - mid


def expander(heads, width):
    row, col = iota((Q, width), 0), iota((Q, width), 1)
    hit = ((row & (heads - 1)) == (col >> 6)) & (row < 4 * heads)
    return jnp.where(hit, 1.0, 0.0).astype(BF)


def mix(tail, x, taps, bias):
    seen = jnp.concatenate([tail, x], axis=0)
    v = bias + taps[3:4] * x
    for back in (1, 2, 3):
        v = v + taps[3 - back : 4 - back] * pltpu.roll(seen, back, 0)[8:]
    return silu(v).astype(BF)


def states_kernel(
    feat, coup, raw, dlog, tapf, offf, tapc, offc, ftail, ctail,
    x_out, cb_out, m_out, lt_out, le_out, d_out, e_out,
    ex, ftl, ctl, acc, dec,
):
    c = pl.program_id(0)
    heads, width = raw.shape[0], feat.shape[1]

    @pl.when(c == 0)
    def _():
        ex[...] = expander(heads, width)
        ftl[...] = ftail[...]
        ctl[...] = ctail[...]
        acc[...] = jnp.zeros_like(acc)
        dec[...] = jnp.ones_like(dec)

    r = raw[...]
    step = jnp.maximum(r, 0.0) + jnp.log1p(jnp.exp(-jnp.abs(r)))
    ld = -jnp.exp(dlog[...]) * step * LOG2E
    upto = jnp.where(iota((Q, Q), 0) <= iota((Q, Q), 1), 1.0, 0.0)
    lc = dot(ld, upto, precision=HI)
    m = lc - jnp.log(step) * LOG2E
    m_out[...] = m
    to_end = jnp.exp2(lc[:, Q - 1 : Q] - m)
    parts = [to_end, *split3(jnp.exp2(lc))]
    if 4 * heads < Q:
        parts.append(jnp.zeros((Q - 4 * heads, Q), F32))
    t1 = jnp.transpose(jnp.concatenate(parts, axis=0))
    lane = iota((Q, Q), 1)
    lte = jnp.where(lane < heads, t1, 0.0).astype(BF)
    le = jnp.where(lane >= heads, t1, 0.0).astype(BF)
    le_out[...] = le
    lt_out[...] = jnp.transpose(jnp.concatenate([lc] * (Q // heads), axis=0))
    spread = jnp.concatenate([lte, le[Q - 16 :]], axis=0)

    halves = []
    for j in range(2):
        sl = slice(j * STATE, (j + 1) * STATE)
        x = coup[:, sl].astype(F32)
        f = mix(ctl[:, sl], x, tapc[:, sl], offc[:, sl])
        cb_out[:, sl] = f
        ctl[:, sl] = x[Q - 8 :]
        halves.append(f)
    bt = jnp.transpose(halves[0].astype(F32)).astype(BF)

    for j in range(width // 256):
        sl = slice(j * 256, (j + 1) * 256)
        x = feat[:, sl].astype(F32)
        f = mix(ftl[:, sl], x, tapf[:, sl], offf[:, sl])
        x_out[:, sl] = f
        ftl[:, sl] = x[Q - 8 :]
        e = dot(spread, ex[:, sl])
        xw = (f.astype(F32) * e[:Q]).astype(BF)
        d = dot(bt, xw)
        row = e[Q + 15 : Q + 16]
        d_out[:, sl] = d.astype(BF)
        acc[:, sl] = acc[:, sl] * row + d
        dec[:, sl] = dec[:, sl] * row

    @pl.when(c == pl.num_programs(0) - 1)
    def _():
        e_out[0:STATE] = acc[...].astype(BF)
        hi, mid, lo = split3(dec[...])
        which = iota(dec.shape, 0)
        rows = jnp.where(which == 0, hi, jnp.where(which == 1, mid, jnp.where(which == 2, lo, 0.0)))
        e_out[STATE : STATE + 16] = jnp.concatenate([rows, jnp.zeros_like(rows)], axis=0).astype(BF)


def inside_kernel(x_ref, cb, m, lt, y_out):
    scores = dot_rows(cb[:, STATE:], cb[:, :STATE])
    causal = iota((Q, Q), 0) >= iota((Q, Q), 1)
    first = jnp.where(iota((Q, Q), 1) < HEAD, 1.0, 0.0)
    mask_a, mask_b = first.astype(BF), (1.0 - first).astype(BF)
    for p in range(x_ref.shape[1] // 128):
        ws = []
        for h in (2 * p, 2 * p + 1):
            decay = jnp.exp2(lt[:, h : h + 1] - m[h : h + 1, :])
            ws.append((jnp.where(causal, decay, 0.0) * scores).astype(BF))
        xp = x_ref[:, p * 128 : (p + 1) * 128]
        both = jnp.concatenate([xp * mask_a, xp * mask_b], axis=0)
        y = dot(jnp.concatenate(ws, axis=1), both)
        y_out[:, p * 128 : (p + 1) * 128] = y.astype(BF)


def carried_kernel(heads, others, *refs):
    recv = refs[:others]
    d, le, cb, y_in, gate, g_out, ss_out, state, ex = refs[others:]
    width = gate.shape[1]

    @pl.when(pl.program_id(0) == 0)
    def _():
        ex[...] = expander(heads, width)
        if others == 0:
            state[...] = jnp.zeros_like(state)
        for j in range(width // 256 if others else 0):
            sl = slice(j * 256, (j + 1) * 256)
            total = jnp.zeros((STATE, 256), F32)
            through = jnp.ones((1, 256), F32)
            for r in recv:
                total = total + through * r[:STATE, sl].astype(F32)
                rows = r[STATE : STATE + 16, sl].astype(F32)
                through = through * (rows[0:1] + rows[1:2] + rows[2:3])
            state[:, sl] = total

    out_map = cb[:, STATE:]
    lev = le[...]
    acc = jnp.zeros((Q, 256), F32)
    for j in range(width // 256):
        sl = slice(j * 256, (j + 1) * 256)
        s = state[:, sl]
        e = dot(lev, ex[:, sl])
        y = y_in[:, sl].astype(F32) + dot(out_map, s.astype(BF)) * e
        g = y * silu(gate[:, sl].astype(F32))
        acc = acc + g * g
        g_out[:, sl] = g.astype(BF)
        state[:, sl] = s * e[Q - 1 : Q] + d[:, sl].astype(F32)
    acc = acc[:, :128] + acc[:, 128:]
    ss_out[0] = dot_rows(jnp.ones((8, Q), F32), acc, precision=HI)


def norm_kernel(ss, g, gain, out):
    c = pl.program_id(0)
    scale = lax.rsqrt(ss[pl.ds(c, 1), :] * (1.0 / INNER) + 1e-5)
    scale = jnp.transpose(jnp.broadcast_to(scale, (Q, Q)))
    for j in range(g.shape[1] // 128):
        sl = slice(j * 128, (j + 1) * 128)
        out[:, sl] = (g[:, sl].astype(F32) * gain[:, sl] * scale).astype(BF)


def passed_along(block, distance):
    devices = range(lax.axis_size("seq"))
    route = [(i - distance, i) for i in devices if i - distance in devices]
    return lax.ppermute(block, "seq", route)


def params():
    return pltpu.CompilerParams(vmem_limit_bytes=VMEM_LIMIT)


def on_device(
    features, coupling, gate_values, step_raw, decay_log,
    feature_taps, feature_offset, coupling_taps, coupling_offset, norm_gain,
):
    tokens, width = features.shape
    heads = decay_log.shape[0]
    blocks = tokens // Q
    seq = lax.axis_size("seq")
    tail = feature_taps.shape[0] - 1
    ends = jnp.concatenate([features[tokens - tail :], coupling[tokens - tail :]], axis=1)
    prior = passed_along(ends, 1)
    prior = jnp.pad(prior, ((8 - tail, 0), (0, 0))).astype(F32)

    def whole(*shape):
        return pl.BlockSpec(shape, lambda c: (0,) * len(shape))

    def rows(n):
        return pl.BlockSpec((Q, n), lambda c: (c, 0))

    cols = pl.BlockSpec((heads, Q), lambda c: (0, c))
    sds = jax.ShapeDtypeStruct
    work = 2 * tokens * width * STATE
    x, cb, m, lt, le, d, end = pl.pallas_call(
        states_kernel,
        grid=(blocks,),
        in_specs=[
            rows(width), rows(2 * STATE), cols, whole(heads, 1), whole(4, width), whole(1, width),
            whole(4, 2 * STATE), whole(1, 2 * STATE), whole(8, width), whole(8, 2 * STATE),
        ],
        out_specs=[
            rows(width), rows(2 * STATE), cols, rows(Q), rows(Q), rows(width),
            whole(STATE + 16, width),
        ],
        out_shape=[
            sds((tokens, width), BF), sds((tokens, 2 * STATE), BF), sds((heads, tokens), F32),
            sds((tokens, Q), F32), sds((tokens, Q), BF), sds((tokens, width), BF),
            sds((STATE + 16, width), BF),
        ],
        scratch_shapes=[
            pltpu.VMEM((Q, width), BF), pltpu.VMEM((8, width), F32),
            pltpu.VMEM((8, 2 * STATE), F32), pltpu.VMEM((STATE, width), F32),
            pltpu.VMEM((8, width), F32),
        ],
        compiler_params=params(),
        cost_estimate=pl.CostEstimate(flops=2 * work, bytes_accessed=6 * tokens * width, transcendentals=0),
        name="states",
    )(
        features, coupling, step_raw, decay_log[:, None], feature_taps, feature_offset[None],
        coupling_taps, coupling_offset[None], prior[:, :width], prior[:, width:],
    )
    recv = [passed_along(end, distance) for distance in range(1, seq)]
    y = pl.pallas_call(
        inside_kernel,
        grid=(blocks,),
        in_specs=[rows(width), rows(2 * STATE), cols, rows(Q)],
        out_specs=rows(width),
        out_shape=sds((tokens, width), BF),
        compiler_params=params(),
        cost_estimate=pl.CostEstimate(flops=8 * work, bytes_accessed=4 * tokens * width, transcendentals=0),
        name="inside",
    )(x, cb, m, lt)
    g, ss = pl.pallas_call(
        functools.partial(carried_kernel, heads, seq - 1),
        grid=(blocks,),
        in_specs=[whole(STATE + 16, width)] * (seq - 1)
        + [rows(width), rows(Q), rows(2 * STATE), rows(width), rows(width)],
        out_specs=[rows(width), pl.BlockSpec((1, 8, Q), lambda c: (c, 0, 0))],
        out_shape=[sds((tokens, width), BF), sds((blocks, 8, Q), F32)],
        scratch_shapes=[pltpu.VMEM((STATE, width), F32), pltpu.VMEM((Q, width), BF)],
        compiler_params=params(),
        cost_estimate=pl.CostEstimate(flops=2 * work, bytes_accessed=8 * tokens * width, transcendentals=0),
        name="carried",
    )(*recv, d, le, cb, y, gate_values)
    squares = lax.psum(ss[:, 0, :], "mp")
    return pl.pallas_call(
        norm_kernel,
        grid=(blocks,),
        in_specs=[whole(blocks, Q), rows(width), whole(1, width)],
        out_specs=rows(width),
        out_shape=sds((tokens, width), BF),
        compiler_params=params(),
        cost_estimate=pl.CostEstimate(flops=2 * tokens * width, bytes_accessed=4 * tokens * width, transcendentals=0),
        name="normalise",
    )(squares, g, norm_gain[None])


def solution(mesh):
    in_specs = (
        P("seq", "mp"), P("seq", None), P("seq", "mp"), P("mp", "seq"), P("mp"),
        P(None, "mp"), P("mp"), P(), P(), P("mp"),
    )
    return jax.shard_map(
        on_device, mesh=mesh, in_specs=in_specs, out_specs=P("seq", "mp"), check_vma=False
    )
```

```python
import functools
import jax
import jax.numpy as jnp
from jax import lax
from jax.sharding import PartitionSpec as P
from jax.experimental import pallas as pl
from jax.experimental.pallas import tpu as pltpu

INNER = 16384
Q = 128
ROWS = 512
STATE = 128
HEAD = 64
LOG2E = 1.4426950408889634
F32 = jnp.float32
BF = jnp.bfloat16
HI = lax.Precision.HIGHEST
VMEM_LIMIT = 60 * 1024 * 1024


def iota(shape, dim):
    return lax.broadcasted_iota(jnp.int32, shape, dim)


def dot(a, b, **kw):
    return jnp.dot(a, b, preferred_element_type=F32, **kw)


def dot_rows(a, b, **kw):
    return lax.dot_general(a, b, (((1,), (1,)), ((), ())), preferred_element_type=F32, **kw)


def silu(v):
    return v * pl.reciprocal(1.0 + jnp.exp2(v * -LOG2E), approx=True)


def split3(v):
    hi = v.astype(BF).astype(F32)
    mid = (v - hi).astype(BF).astype(F32)
    return hi, mid, (v - hi) - mid


def expander(heads, width, first_head):
    row, col = iota((Q, width), 0), iota((Q, width), 1)
    hit = ((row & (heads - 1)) == (col >> 6) + first_head) & (row < 4 * heads)
    return jnp.where(hit, 1.0, 0.0).astype(BF)


def mix(tail, x, taps, bias):
    seen = jnp.concatenate([tail, x], axis=0)
    v = bias + taps[3:4] * x
    for back in (1, 2, 3):
        v = v + taps[3 - back : 4 - back] * pltpu.roll(seen, back, 0)[8:]
    return silu(v).astype(BF)


def prepare_kernel(raw, dlog, m_out, lt_out, le_out, lte_out):
    heads, tokens = raw.shape
    blocks = tokens // Q
    r = jnp.concatenate([raw[:, c * Q : (c + 1) * Q] for c in range(blocks)], axis=0)
    step = jnp.maximum(r, 0.0) + jnp.log1p(jnp.exp(-jnp.abs(r)))
    rate = jnp.broadcast_to(jnp.exp(dlog[...]) * -LOG2E, (heads, Q))
    ld = jnp.concatenate([rate] * blocks, axis=0) * step
    upto = jnp.where(iota((Q, Q), 0) <= iota((Q, Q), 1), 1.0, 0.0)
    lc = dot(ld, upto, precision=HI)
    m = lc - jnp.log(step) * LOG2E
    to_end = jnp.exp2(lc[:, Q - 1 : Q] - m)
    pieces = split3(jnp.exp2(lc))
    lane = iota((Q, Q), 1)
    for c in range(blocks):
        sl, rs = slice(c * Q, (c + 1) * Q), slice(c * heads, (c + 1) * heads)
        m_out[:, sl] = m[rs]
        parts = [to_end[rs], *(piece[rs] for piece in pieces)]
        if 4 * heads < Q:
            parts.append(jnp.zeros((Q - 4 * heads, Q), F32))
        t1 = jnp.transpose(jnp.concatenate(parts, axis=0))
        lte_out[sl] = jnp.where(lane < heads, t1, 0.0).astype(BF)
        le_out[sl] = jnp.where(lane >= heads, t1, 0.0).astype(BF)
        lt_out[sl] = jnp.transpose(jnp.concatenate([lc[rs]] * (Q // heads), axis=0))


def exchange(n, src, dst, send_sem, recv_sem):
    me = lax.axis_index("seq")

    def copy(d):
        return pltpu.make_async_remote_copy(
            src_ref=src, dst_ref=dst.at[d - 1], send_sem=send_sem.at[d - 1], recv_sem=recv_sem.at[d - 1],
            device_id={"seq": lax.rem(me + d, n)}, device_id_type=pl.DeviceIdType.MESH,
        )

    @pl.when(pl.program_id(0) == 0)
    def _():
        barrier = pltpu.get_barrier_semaphore()
        for d in range(1, n):
            pl.semaphore_signal(
                barrier, inc=1, device_id={"seq": lax.rem(me + d, n)}, device_id_type=pl.DeviceIdType.MESH
            )
        pl.semaphore_wait(barrier, n - 1)
        for d in range(1, n):
            pl.when(me + d < n)(lambda d=d: copy(d).start())

    def finish():
        @pl.when(pl.program_id(0) == pl.num_programs(0) - 1)
        def _():
            for d in range(1, n):
                pl.when(me + d < n)(lambda d=d: copy(d).wait_send())
                pl.when(me >= d)(lambda d=d: copy(d).wait_recv())

    return finish


def chunks(ref):
    return ref.shape[0] // Q


def rows_of(i):
    return pl.ds(pl.multiple_of(i * Q, Q), Q)


def states_body(first_head, heads, feat, lte, le, taps, off, ftail, input_map, x_out, d_out, e_out, ex, ftl, acc, dec):
    c = pl.program_id(0)
    width = feat.shape[1]

    @pl.when(c == 0)
    def _():
        ex[...] = expander(heads, width, first_head)
        ftl[...] = ftail[...]
        acc[...] = jnp.zeros_like(acc)
        dec[...] = jnp.ones_like(dec)

    def one(i, carry):
        rs = rows_of(i)
        bt = jnp.transpose(input_map(rs).astype(F32)).astype(BF)
        ends = le[pl.ds(pl.multiple_of(i * Q + Q - 16, 16), 16), :]
        spread = jnp.concatenate([lte[rs, :], ends], axis=0)
        for j in range(width // 256):
            sl = slice(j * 256, (j + 1) * 256)
            e = dot(spread, ex[:, sl])
            xw = []
            for k in range(2):
                at = slice(j * 256 + k * 128, j * 256 + (k + 1) * 128)
                x = feat[rs, at].astype(F32)
                f = mix(ftl[:, at], x, taps[:, at], off[:, at])
                x_out[rs, at] = f
                ftl[:, at] = x[Q - 8 :]
                xw.append((f.astype(F32) * e[:Q, k * 128 : (k + 1) * 128]).astype(BF))
            d = dot(bt, jnp.concatenate(xw, axis=1))
            row = e[Q + 15 : Q + 16]
            d_out[rs, sl] = d.astype(BF)
            acc[:, sl] = acc[:, sl] * row + d
            dec[:, sl] = dec[:, sl] * row
        return carry

    lax.fori_loop(0, chunks(feat), one, 0)

    @pl.when(c == pl.num_programs(0) - 1)
    def _():
        e_out[0:STATE] = acc[...].astype(BF)
        hi, mid, lo = split3(dec[...])
        which = iota(dec.shape, 0)
        rows = jnp.where(which == 0, hi, jnp.where(which == 1, mid, jnp.where(which == 2, lo, 0.0)))
        e_out[STATE : STATE + 16] = jnp.concatenate([rows, jnp.zeros_like(rows)], axis=0).astype(BF)


def states_a_kernel(
    heads, feat, lte, le, taps, off, ftail, coup, tapc, offc, ctail, x_out, d_out, e_out, cb_out, ex, ftl, acc, dec, ctl
):
    @pl.when(pl.program_id(0) == 0)
    def _():
        ctl[...] = ctail[...]

    def input_map(rs):
        for j in (1, 0):
            sl = slice(j * STATE, (j + 1) * STATE)
            x = coup[rs, sl].astype(F32)
            f = mix(ctl[:, sl], x, tapc[:, sl], offc[:, sl])
            cb_out[rs, sl] = f
            ctl[:, sl] = x[Q - 8 :]
        return f

    states_body(0, heads, feat, lte, le, taps, off, ftail, input_map, x_out, d_out, e_out, ex, ftl, acc, dec)


def states_b_kernel(
    heads, n, feat, lte, le, taps, off, ftail, cb, e_a, x_out, d_out, e_out, recv, ex, ftl, acc, dec, send_sem, recv_sem
):
    finish = exchange(n, e_a, recv, send_sem, recv_sem)
    states_body(
        heads // 2, heads, feat, lte, le, taps, off, ftail, lambda rs: cb[rs, :STATE],
        x_out, d_out, e_out, ex, ftl, acc, dec,
    )
    finish()


def inside_kernel(n, x_a, x_b, cb, m, lt, e_b, y_out, recv, send_sem, recv_sem):
    finish = exchange(n, e_b, recv, send_sem, recv_sem)
    causal = iota((Q, Q), 0) >= iota((Q, Q), 1)
    first = jnp.where(iota((Q, Q), 1) < HEAD, 1.0, 0.0)
    mask_a, mask_b = first.astype(BF), (1.0 - first).astype(BF)
    half = x_a.shape[1] // 128

    def one(i, carry):
        rs = rows_of(i)
        scores = dot_rows(cb[rs, STATE:], cb[rs, :STATE])
        for p in range(2 * half):
            ws = []
            for h in (2 * p, 2 * p + 1):
                decay = jnp.exp2(lt[rs, h : h + 1] - m[h : h + 1, rs])
                ws.append((jnp.where(causal, decay, 0.0) * scores).astype(BF))
            x = x_a if p < half else x_b
            xp = x[rs, (p % half) * 128 : (p % half + 1) * 128]
            both = jnp.concatenate([xp * mask_a, xp * mask_b], axis=0)
            y = dot(jnp.concatenate(ws, axis=1), both)
            y_out[rs, p * 128 : (p + 1) * 128] = y.astype(BF)
        return carry

    lax.fori_loop(0, chunks(x_a), one, 0)
    finish()


def carried_kernel(heads, others, place, recv_a, recv_b, d_a, d_b, le, cb, y_in, gate, g_out, ss_out, state, ex):
    width = gate.shape[1]
    half = width // 2
    c = pl.program_id(0)

    @pl.when(c == 0)
    def _():
        ex[...] = expander(heads, width, 0)
        for j in range(width // 256):
            recv, at = (recv_a, j * 256) if j * 256 < half else (recv_b, j * 256 - half)
            total = jnp.zeros((STATE, 256), F32)
            through = jnp.ones((1, 256), F32)
            for d in range(others):
                came = place[0] > d
                end = recv[d, :STATE, at : at + 256].astype(F32)
                rows = recv[d, STATE : STATE + 16, at : at + 256].astype(F32)
                total = total + jnp.where(came, through * end, 0.0)
                through = jnp.where(came, through * (rows[0:1] + rows[1:2] + rows[2:3]), 0.0)
            state[:, j * 256 : (j + 1) * 256] = total

    def one(i, carry):
        rs = rows_of(i)
        out_map = cb[rs, STATE:]
        lev = le[rs, :]
        acc = jnp.zeros((Q, 128), F32)
        for j in range(width // 256):
            sl = slice(j * 256, (j + 1) * 256)
            d, at = (d_a, j * 256) if j * 256 < half else (d_b, j * 256 - half)
            s = state[:, sl]
            e = dot(lev, ex[:, sl])
            new = dot(out_map, s.astype(BF)) * e
            state[:, sl] = s * e[Q - 1 : Q] + d[rs, at : at + 256].astype(F32)
            for k in range(2):
                part = slice(j * 256 + k * 128, j * 256 + (k + 1) * 128)
                y = y_in[rs, part].astype(F32) + new[:, k * 128 : (k + 1) * 128]
                g = y * silu(gate[rs, part].astype(F32))
                acc = acc + g * g
                g_out[rs, part] = g.astype(BF)
        ss = dot_rows(jnp.ones((8, Q), F32), acc, precision=HI)
        ss_out[pl.ds(c * chunks(gate) + i, 1), :] = ss[0:1]
        return carry

    lax.fori_loop(0, chunks(gate), one, 0)


def sums_kernel(n, ss, out, slots, send_sem, recv_sem):
    me = lax.axis_index("mp")

    def copy(d):
        return pltpu.make_async_remote_copy(
            src_ref=ss, dst_ref=slots.at[d - 1], send_sem=send_sem.at[d - 1], recv_sem=recv_sem.at[d - 1],
            device_id={"mp": lax.rem(me + d, n)}, device_id_type=pl.DeviceIdType.MESH,
        )

    barrier = pltpu.get_barrier_semaphore()
    for d in range(1, n):
        pl.semaphore_signal(
            barrier, inc=1, device_id={"mp": lax.rem(me + d, n)}, device_id_type=pl.DeviceIdType.MESH
        )
    pl.semaphore_wait(barrier, n - 1)
    for d in range(1, n):
        copy(d).start()
    total = ss[...]
    for d in range(1, n):
        copy(d).wait()
        total = total + slots[d - 1]
    out[...] = total


def norm_kernel(ss, g, gain, out):
    c = pl.program_id(0)

    def one(i, carry):
        rs = rows_of(i)
        scale = lax.rsqrt(ss[pl.ds(c * chunks(g) + i, 1), :] * (1.0 / INNER) + 1e-5)
        scale = jnp.transpose(jnp.broadcast_to(scale, (Q, Q)))
        for j in range(g.shape[1] // 128):
            sl = slice(j * 128, (j + 1) * 128)
            out[rs, sl] = (g[rs, sl].astype(F32) * gain[:, sl] * scale).astype(BF)
        return carry

    lax.fori_loop(0, chunks(g), one, 0)


def passed_along(block, distance):
    devices = range(lax.axis_size("seq"))
    route = [(i - distance, i) for i in devices if i - distance in devices]
    return lax.ppermute(block, "seq", route)


def params(**kw):
    return pltpu.CompilerParams(vmem_limit_bytes=VMEM_LIMIT, **kw)


def on_device(
    features, coupling, gate_values, step_raw, decay_log,
    feature_taps, feature_offset, coupling_taps, coupling_offset, norm_gain,
):
    tokens, width = features.shape
    heads = decay_log.shape[0]
    blocks = tokens // Q
    grid = (tokens // ROWS,)
    half = width // 2
    seq, mp = lax.axis_size("seq"), lax.axis_size("mp")
    tail = feature_taps.shape[0] - 1
    ends = jnp.concatenate([features[tokens - tail :], coupling[tokens - tail :]], axis=1)
    prior = passed_along(ends, 1)
    prior = jnp.pad(prior, ((8 - tail, 0), (0, 0))).astype(F32)

    def whole(*shape):
        return pl.BlockSpec(shape, lambda c: (0,) * len(shape))

    def rows(n, at=0):
        return pl.BlockSpec((ROWS, n), lambda c: (c, at))

    def side(n, at):
        return pl.BlockSpec((n, half), lambda c: (0, at))

    hbm = pl.BlockSpec(memory_space=pl.ANY)
    vmem = pl.BlockSpec(memory_space=pltpu.VMEM)
    sds = jax.ShapeDtypeStruct
    work = 2 * tokens * width * STATE

    def cost(flops, moved):
        return pl.CostEstimate(flops=flops, bytes_accessed=moved * tokens * width, transcendentals=0)

    m, lt, le, lte = pl.pallas_call(
        prepare_kernel,
        in_specs=[vmem, vmem],
        out_specs=[vmem] * 4,
        out_shape=[
            sds((heads, tokens), F32), sds((tokens, Q), F32), sds((tokens, Q), BF), sds((tokens, Q), BF),
        ],
        compiler_params=params(),
        cost_estimate=pl.CostEstimate(flops=work // 64, bytes_accessed=tokens * 1024, transcendentals=0),
        name="prepare",
    )(step_raw, decay_log[:, None])

    part = sds((tokens, half), BF)
    end_shape = sds((STATE + 16, half), BF)
    recv_shape = sds((seq - 1, STATE + 16, half), BF)
    keep = [
        pltpu.VMEM((Q, half), BF), pltpu.VMEM((8, half), F32),
        pltpu.VMEM((STATE, half), F32), pltpu.VMEM((8, half), F32),
    ]
    sems = [pltpu.SemaphoreType.DMA((seq - 1,)), pltpu.SemaphoreType.DMA((seq - 1,))]

    def state_specs(at):
        return [rows(half, at), rows(Q), rows(Q), side(4, at), side(1, at), side(8, at)]

    state_args = (features, lte, le, feature_taps, feature_offset[None], prior)
    x_a, d_a, e_a, cb = pl.pallas_call(
        functools.partial(states_a_kernel, heads),
        grid=grid,
        in_specs=state_specs(0)
        + [rows(2 * STATE), whole(4, 2 * STATE), whole(1, 2 * STATE), pl.BlockSpec((8, 2 * STATE), lambda c: (0, width // (2 * STATE)))],
        out_specs=[rows(half), rows(half), whole(STATE + 16, half), rows(2 * STATE)],
        out_shape=[part, part, end_shape, sds((tokens, 2 * STATE), BF)],
        scratch_shapes=keep + [pltpu.VMEM((8, 2 * STATE), F32)],
        compiler_params=params(),
        cost_estimate=cost(work, 3),
        name="states_a",
    )(*state_args, coupling, coupling_taps, coupling_offset[None], prior)
    x_b, d_b, e_b, recv_a = pl.pallas_call(
        functools.partial(states_b_kernel, heads, seq),
        grid=grid,
        in_specs=state_specs(1) + [rows(2 * STATE), hbm],
        out_specs=[rows(half), rows(half), whole(STATE + 16, half), hbm],
        out_shape=[part, part, end_shape, recv_shape],
        scratch_shapes=keep + sems,
        compiler_params=params(collective_id=0, has_side_effects=True),
        cost_estimate=cost(work, 3),
        name="states_b",
    )(*state_args, cb, e_a)
    y, recv_b = pl.pallas_call(
        functools.partial(inside_kernel, seq),
        grid=grid,
        in_specs=[rows(half), rows(half), rows(2 * STATE), pl.BlockSpec((heads, ROWS), lambda c: (0, c)), rows(Q), hbm],
        out_specs=[rows(width), hbm],
        out_shape=[sds((tokens, width), BF), recv_shape],
        scratch_shapes=sems,
        compiler_params=params(collective_id=1, has_side_effects=True),
        cost_estimate=cost(4 * work, 4),
        name="inside",
    )(x_a, x_b, cb, m, lt, e_b)
    g, ss = pl.pallas_call(
        functools.partial(carried_kernel, heads, seq - 1),
        grid=grid,
        in_specs=[
            pl.BlockSpec(memory_space=pltpu.SMEM),
            whole(seq - 1, STATE + 16, half), whole(seq - 1, STATE + 16, half),
            rows(half), rows(half), rows(Q), rows(2 * STATE), rows(width), rows(width),
        ],
        out_specs=[rows(width), whole(blocks, Q)],
        out_shape=[sds((tokens, width), BF), sds((blocks, Q), F32)],
        scratch_shapes=[pltpu.VMEM((STATE, width), F32), pltpu.VMEM((Q, width), BF)],
        compiler_params=params(),
        cost_estimate=cost(2 * work, 8),
        name="carried",
    )(lax.axis_index("seq").reshape(1), recv_a, recv_b, d_a, d_b, le, cb, y, gate_values)
    squares = pl.pallas_call(
        functools.partial(sums_kernel, mp),
        in_specs=[vmem],
        out_specs=vmem,
        out_shape=sds((blocks, Q), F32),
        scratch_shapes=[
            pltpu.VMEM((mp - 1, blocks, Q), F32),
            pltpu.SemaphoreType.DMA((mp - 1,)), pltpu.SemaphoreType.DMA((mp - 1,)),
        ],
        compiler_params=params(collective_id=2, has_side_effects=True),
        name="sums",
    )(ss)
    return pl.pallas_call(
        norm_kernel,
        grid=grid,
        in_specs=[whole(blocks, Q), rows(width), whole(1, width)],
        out_specs=rows(width),
        out_shape=sds((tokens, width), BF),
        compiler_params=params(),
        cost_estimate=cost(2 * tokens * width, 4),
        name="normalise",
    )(squares, g, norm_gain[None])


def solution(mesh):
    in_specs = (
        P("seq", "mp"), P("seq", None), P("seq", "mp"), P("mp", "seq"), P("mp"),
        P(None, "mp"), P("mp"), P(), P(), P("mp"),
    )
    return jax.shard_map(
        on_device, mesh=mesh, in_specs=in_specs, out_specs=P("seq", "mp"), check_vma=False
    )
```

```python
import functools
import jax
import jax.numpy as jnp
from jax import lax
from jax.sharding import PartitionSpec as P
from jax.experimental import pallas as pl
from jax.experimental.pallas import tpu as pltpu

INNER = 16384
Q = 128
ROWS = 512
SHORT = 256
STATE = 128
HEAD = 64
LOG2E = 1.4426950408889634
F32 = jnp.float32
BF = jnp.bfloat16
HI = lax.Precision.HIGHEST
VMEM_LIMIT = 60 * 1024 * 1024


def iota(shape, dim):
    return lax.broadcasted_iota(jnp.int32, shape, dim)


def dot(a, b, **kw):
    return jnp.dot(a, b, preferred_element_type=F32, **kw)


def dot_rows(a, b, **kw):
    return lax.dot_general(a, b, (((1,), (1,)), ((), ())), preferred_element_type=F32, **kw)


def silu(v):
    return v * pl.reciprocal(1.0 + jnp.exp2(v * -LOG2E), approx=True)


def split3(v):
    hi = v.astype(BF).astype(F32)
    mid = (v - hi).astype(BF).astype(F32)
    return hi, mid, (v - hi) - mid


def over_channels(by_token, rs, h, first):
    return jnp.where(first, by_token[rs, h : h + 1], by_token[rs, h + 1 : h + 2])


def mix(tail, x, taps, bias):
    seen = jnp.concatenate([tail, x], axis=0)
    v = bias + taps[3:4] * x
    for back in (1, 2, 3):
        v = v + taps[3 - back : 4 - back] * pltpu.roll(seen, back, 0)[8:]
    return silu(v).astype(BF)


def prepare_kernel(raw, dlog, m_out, by_token, rows_out):
    heads, tokens = raw.shape
    blocks = tokens // Q
    r = jnp.concatenate([raw[:, c * Q : (c + 1) * Q] for c in range(blocks)], axis=0)
    step = jnp.maximum(r, 0.0) + jnp.log1p(jnp.exp(-jnp.abs(r)))
    same = iota((heads, heads), 0) == iota((heads, heads), 1)
    dlog_col = jnp.sum(jnp.where(same, dlog[...], 0.0), axis=1, keepdims=True)
    rate = jnp.broadcast_to(jnp.exp(dlog_col) * -LOG2E, (heads, Q))
    ld = jnp.concatenate([rate] * blocks, axis=0) * step
    upto = jnp.where(iota((Q, Q), 0) <= iota((Q, Q), 1), 1.0, 0.0)
    lc = dot(ld, upto, precision=HI)
    m = lc - jnp.log(step) * LOG2E
    to_end = jnp.exp2(lc[:, Q - 1 : Q] - m)
    decay = jnp.exp2(lc)
    ends = []
    for c in range(blocks):
        sl, rs = slice(c * Q, (c + 1) * Q), slice(c * heads, (c + 1) * heads)
        m_out[:, sl] = m[rs]
        parts = [lc[rs], to_end[rs], decay[rs], jnp.zeros((Q - 3 * heads, Q), F32)]
        turned = jnp.transpose(jnp.concatenate(parts, axis=0))
        by_token[sl] = turned
        ends.append(turned[Q - 1 : Q])
    ends = jnp.concatenate(ends, axis=0)
    lane = iota(ends.shape, 1)
    ends = jnp.where((lane >= 2 * heads) & (lane < 3 * heads), ends, 0.0)
    width = rows_out.shape[1]
    row, col = iota((Q, width), 0), iota((Q, width), 1)
    spread = jnp.where(row == (col >> 6) + 2 * heads, 1.0, 0.0).astype(BF)
    hi, mid, lo = (piece.astype(BF) for piece in split3(ends))
    rows_out[...] = dot(hi, spread) + dot(mid, spread) + dot(lo, spread)


def exchange(n, src, dst, send_sem, recv_sem):
    me = lax.axis_index("seq")

    def copy(d):
        return pltpu.make_async_remote_copy(
            src_ref=src, dst_ref=dst.at[d - 1], send_sem=send_sem.at[d - 1], recv_sem=recv_sem.at[d - 1],
            device_id={"seq": lax.rem(me + d, n)}, device_id_type=pl.DeviceIdType.MESH,
        )

    @pl.when(pl.program_id(0) == 0)
    def _():
        barrier = pltpu.get_barrier_semaphore()
        for d in range(1, n):
            pl.semaphore_signal(
                barrier, inc=1, device_id={"seq": lax.rem(me + d, n)}, device_id_type=pl.DeviceIdType.MESH
            )
        pl.semaphore_wait(barrier, n - 1)
        for d in range(1, n):
            pl.when(me + d < n)(lambda d=d: copy(d).start())

    def finish():
        @pl.when(pl.program_id(0) == pl.num_programs(0) - 1)
        def _():
            for d in range(1, n):
                pl.when(me + d < n)(lambda d=d: copy(d).wait_send())
                pl.when(me >= d)(lambda d=d: copy(d).wait_recv())

    return finish


def chunks(ref):
    return ref.shape[0] // Q


def rows_of(i):
    return pl.ds(pl.multiple_of(i * Q, Q), Q)


def states_body(first_head, heads, feat, by_token, decay, taps, off, ftail, input_map, x_out, d_out, e_out, ftl, acc, dec):
    c = pl.program_id(0)
    width = feat.shape[1]

    @pl.when(c == 0)
    def _():
        ftl[...] = ftail[...]
        acc[...] = jnp.zeros_like(acc)
        dec[...] = jnp.ones_like(dec)

    def one(i, carry):
        rs = rows_of(i)
        first = iota((Q, 128), 1) < HEAD
        row = decay[pl.ds(c * chunks(feat) + i, 1), :]
        bt = jnp.transpose(input_map(rs).astype(F32)).astype(BF)
        for j in range(width // 256):
            sl = slice(j * 256, (j + 1) * 256)
            xw = []
            for k in range(2):
                at = slice(j * 256 + k * 128, j * 256 + (k + 1) * 128)
                x = feat[rs, at].astype(F32)
                f = mix(ftl[:, at], x, taps[:, at], off[:, at])
                x_out[rs, at] = f
                ftl[:, at] = x[Q - 8 :]
                e = over_channels(by_token, rs, heads + first_head + 2 * (2 * j + k), first)
                xw.append((f.astype(F32) * e).astype(BF))
            d = dot(bt, jnp.concatenate(xw, axis=1))
            d_out[rs, sl] = d.astype(BF)
            acc[:, sl] = acc[:, sl] * row[:, sl] + d
        dec[...] = dec[...] * row
        return carry

    lax.fori_loop(0, chunks(feat), one, 0)

    @pl.when(c == pl.num_programs(0) - 1)
    def _():
        e_out[0:STATE] = acc[...].astype(BF)
        hi, mid, lo = split3(dec[...])
        which = iota(dec.shape, 0)
        rows = jnp.where(which == 0, hi, jnp.where(which == 1, mid, jnp.where(which == 2, lo, 0.0)))
        e_out[STATE : STATE + 16] = jnp.concatenate([rows, jnp.zeros_like(rows)], axis=0).astype(BF)


def states_a_kernel(
    heads, feat, by_token, decay, taps, off, ftail, coup, tapc, offc, ctail, x_out, d_out, e_out, cb_out, ftl, acc, dec, ctl
):
    @pl.when(pl.program_id(0) == 0)
    def _():
        ctl[...] = ctail[...]

    def input_map(rs):
        for j in (1, 0):
            sl = slice(j * STATE, (j + 1) * STATE)
            x = coup[rs, sl].astype(F32)
            f = mix(ctl[:, sl], x, tapc[:, sl], offc[:, sl])
            cb_out[rs, sl] = f
            ctl[:, sl] = x[Q - 8 :]
        return f

    states_body(0, heads, feat, by_token, decay, taps, off, ftail, input_map, x_out, d_out, e_out, ftl, acc, dec)


def states_b_kernel(
    heads, n, feat, by_token, decay, taps, off, ftail, cb, e_a, x_out, d_out, e_out, recv, ftl, acc, dec, send_sem, recv_sem
):
    finish = exchange(n, e_a, recv, send_sem, recv_sem)
    states_body(
        heads // 2, heads, feat, by_token, decay, taps, off, ftail, lambda rs: cb[rs, :STATE],
        x_out, d_out, e_out, ftl, acc, dec,
    )
    finish()


def inside_kernel(n, x_a, x_b, cb, m, lt, e_b, y_out, recv, send_sem, recv_sem):
    finish = exchange(n, e_b, recv, send_sem, recv_sem)
    causal = iota((Q, Q), 0) >= iota((Q, Q), 1)
    first = jnp.where(iota((Q, Q), 1) < HEAD, 1.0, 0.0)
    mask_a, mask_b = first.astype(BF), (1.0 - first).astype(BF)
    half = x_a.shape[1] // 128

    def one(i, carry):
        rs = rows_of(i)
        scores = dot_rows(cb[rs, STATE:], cb[rs, :STATE])
        for p in range(2 * half):
            ws = []
            for h in (2 * p, 2 * p + 1):
                decay = jnp.exp2(lt[rs, h : h + 1] - m[h : h + 1, rs])
                ws.append((jnp.where(causal, decay, 0.0) * scores).astype(BF))
            x = x_a if p < half else x_b
            xp = x[rs, (p % half) * 128 : (p % half + 1) * 128]
            both = jnp.concatenate([xp * mask_a, xp * mask_b], axis=0)
            y = dot(jnp.concatenate(ws, axis=1), both)
            y_out[rs, p * 128 : (p + 1) * 128] = y.astype(BF)
        return carry

    lax.fori_loop(0, chunks(x_a), one, 0)
    finish()


def carried_kernel(
    heads, others, n, recv_a, recv_b, d_a, d_b, by_token, decay, cb, y_in, gate,
    g_out, ss_out, state, ss, slots, send_sem, recv_sem,
):
    width = gate.shape[1]
    half = width // 2
    c = pl.program_id(0)
    section, me = lax.axis_index("seq"), lax.axis_index("mp")

    def copy(d):
        return pltpu.make_async_remote_copy(
            src_ref=ss, dst_ref=slots.at[d - 1], send_sem=send_sem.at[d - 1], recv_sem=recv_sem.at[d - 1],
            device_id={"mp": lax.rem(me + d, n)}, device_id_type=pl.DeviceIdType.MESH,
        )

    @pl.when(c == 0)
    def _():
        barrier = pltpu.get_barrier_semaphore()
        for d in range(1, n):
            pl.semaphore_signal(
                barrier, inc=1, device_id={"mp": lax.rem(me + d, n)}, device_id_type=pl.DeviceIdType.MESH
            )
        pl.semaphore_wait(barrier, n - 1)
        for j in range(width // 256):
            recv, at = (recv_a, j * 256) if j * 256 < half else (recv_b, j * 256 - half)
            total = jnp.zeros((STATE, 256), F32)
            through = jnp.ones((1, 256), F32)
            for d in range(others):
                came = section > d
                end = recv[d, :STATE, at : at + 256].astype(F32)
                rows = recv[d, STATE : STATE + 16, at : at + 256].astype(F32)
                total = total + jnp.where(came, through * end, 0.0)
                through = jnp.where(came, through * (rows[0:1] + rows[1:2] + rows[2:3]), 0.0)
            state[:, j * 256 : (j + 1) * 256] = total

    def one(i, carry):
        rs = rows_of(i)
        first = iota((Q, 128), 1) < HEAD
        out_map = cb[rs, STATE:]
        row = decay[pl.ds(c * chunks(gate) + i, 1), :]
        acc = jnp.zeros((Q, 128), F32)
        for j in range(width // 256):
            sl = slice(j * 256, (j + 1) * 256)
            d, at = (d_a, j * 256) if j * 256 < half else (d_b, j * 256 - half)
            s = state[:, sl]
            new = dot(out_map, s.astype(BF))
            state[:, sl] = s * row[:, sl] + d[rs, at : at + 256].astype(F32)
            for k in range(2):
                part = slice(j * 256 + k * 128, j * 256 + (k + 1) * 128)
                e = over_channels(by_token, rs, 2 * heads + 2 * (2 * j + k), first)
                y = y_in[rs, part].astype(F32) + new[:, k * 128 : (k + 1) * 128] * e
                g = y * silu(gate[rs, part].astype(F32))
                acc = acc + g * g
                g_out[rs, part] = g.astype(BF)
        squares = dot_rows(jnp.ones((8, Q), F32), acc, precision=HI)
        ss[pl.ds(c * chunks(gate) + i, 1), :] = squares[0:1]
        return carry

    lax.fori_loop(0, chunks(gate), one, 0)

    @pl.when(c == pl.num_programs(0) - 1)
    def _():
        for d in range(1, n):
            copy(d).start()
        total = ss[...]
        for d in range(1, n):
            copy(d).wait()
            total = total + slots[d - 1]
        ss_out[...] = total


def norm_kernel(ss, g, gain, out):
    c = pl.program_id(0)

    def one(i, carry):
        rs = rows_of(i)
        scale = lax.rsqrt(ss[pl.ds(c * chunks(g) + i, 1), :] * (1.0 / INNER) + 1e-5)
        scale = jnp.transpose(jnp.broadcast_to(scale, (Q, Q)))
        for j in range(g.shape[1] // 128):
            sl = slice(j * 128, (j + 1) * 128)
            out[rs, sl] = (g[rs, sl].astype(F32) * gain[:, sl] * scale).astype(BF)
        return carry

    lax.fori_loop(0, chunks(g), one, 0)


def passed_along(block, distance):
    devices = range(lax.axis_size("seq"))
    route = [(i - distance, i) for i in devices if i - distance in devices]
    return lax.ppermute(block, "seq", route)


def params(**kw):
    return pltpu.CompilerParams(vmem_limit_bytes=VMEM_LIMIT, **kw)


def on_device(
    features, coupling, gate_values, step_raw, decay_log,
    feature_taps, feature_offset, coupling_taps, coupling_offset, norm_gain,
):
    tokens, width = features.shape
    heads = decay_log.shape[0]
    blocks = tokens // Q
    grid = (tokens // ROWS,)
    half = width // 2
    seq, mp = lax.axis_size("seq"), lax.axis_size("mp")
    tail = feature_taps.shape[0] - 1
    ends = jnp.concatenate([features[tokens - tail :], coupling[tokens - tail :]], axis=1)
    prior = passed_along(ends, 1)
    prior = jnp.pad(prior, ((8 - tail, 0), (0, 0))).astype(F32)

    def whole(*shape):
        return pl.BlockSpec(shape, lambda c: (0,) * len(shape))

    def rows(n, at=0):
        return pl.BlockSpec((ROWS, n), lambda c: (c, at))

    def short(n):
        return pl.BlockSpec((SHORT, n), lambda c: (c, 0))

    def side(n, at):
        return pl.BlockSpec((n, half), lambda c: (0, at))

    hbm = pl.BlockSpec(memory_space=pl.ANY)
    vmem = pl.BlockSpec(memory_space=pltpu.VMEM)
    sds = jax.ShapeDtypeStruct
    work = 2 * tokens * width * STATE

    def cost(flops, moved):
        return pl.CostEstimate(flops=flops, bytes_accessed=moved * tokens * width, transcendentals=0)

    m, by_token, decay = pl.pallas_call(
        prepare_kernel,
        in_specs=[vmem, vmem],
        out_specs=[vmem] * 3,
        out_shape=[sds((heads, tokens), F32), sds((tokens, Q), F32), sds((blocks, width), F32)],
        compiler_params=params(),
        cost_estimate=pl.CostEstimate(flops=work // 64, bytes_accessed=tokens * 1024, transcendentals=0),
        name="prepare",
    )(step_raw, decay_log[None])

    part = sds((tokens, half), BF)
    end_shape = sds((STATE + 16, half), BF)
    recv_shape = sds((seq - 1, STATE + 16, half), BF)
    keep = [
        pltpu.VMEM((8, half), F32),
        pltpu.VMEM((STATE, half), F32), pltpu.VMEM((8, half), F32),
    ]
    sems = [pltpu.SemaphoreType.DMA((seq - 1,)), pltpu.SemaphoreType.DMA((seq - 1,))]

    def state_specs(at):
        return [rows(half, at), rows(Q), side(blocks, at), side(4, at), side(1, at), side(8, at)]

    state_args = (features, by_token, decay, feature_taps, feature_offset[None], prior)
    x_a, d_a, e_a, cb = pl.pallas_call(
        functools.partial(states_a_kernel, heads),
        grid=grid,
        in_specs=state_specs(0)
        + [rows(2 * STATE), whole(4, 2 * STATE), whole(1, 2 * STATE), pl.BlockSpec((8, 2 * STATE), lambda c: (0, width // (2 * STATE)))],
        out_specs=[rows(half), rows(half), whole(STATE + 16, half), rows(2 * STATE)],
        out_shape=[part, part, end_shape, sds((tokens, 2 * STATE), BF)],
        scratch_shapes=keep + [pltpu.VMEM((8, 2 * STATE), F32)],
        compiler_params=params(),
        cost_estimate=cost(work, 3),
        name="states_a",
    )(*state_args, coupling, coupling_taps, coupling_offset[None], prior)
    x_b, d_b, e_b, recv_a = pl.pallas_call(
        functools.partial(states_b_kernel, heads, seq),
        grid=grid,
        in_specs=state_specs(1) + [rows(2 * STATE), hbm],
        out_specs=[rows(half), rows(half), whole(STATE + 16, half), hbm],
        out_shape=[part, part, end_shape, recv_shape],
        scratch_shapes=keep + sems,
        compiler_params=params(collective_id=0, has_side_effects=True),
        cost_estimate=cost(work, 3),
        name="states_b",
    )(*state_args, cb, e_a)
    y, recv_b = pl.pallas_call(
        functools.partial(inside_kernel, seq),
        grid=grid,
        in_specs=[rows(half), rows(half), rows(2 * STATE), pl.BlockSpec((heads, ROWS), lambda c: (0, c)), rows(Q), hbm],
        out_specs=[rows(width), hbm],
        out_shape=[sds((tokens, width), BF), recv_shape],
        scratch_shapes=sems,
        compiler_params=params(collective_id=1, has_side_effects=True),
        cost_estimate=cost(4 * work, 4),
        name="inside",
    )(x_a, x_b, cb, m, by_token, e_b)
    g, squares = pl.pallas_call(
        functools.partial(carried_kernel, heads, seq - 1, mp),
        grid=(tokens // SHORT,),
        in_specs=[
            whole(seq - 1, STATE + 16, half), whole(seq - 1, STATE + 16, half),
            short(half), short(half), short(Q), whole(blocks, width), short(2 * STATE), short(width), short(width),
        ],
        out_specs=[short(width), whole(blocks, Q)],
        out_shape=[sds((tokens, width), BF), sds((blocks, Q), F32)],
        scratch_shapes=[
            pltpu.VMEM((STATE, width), F32), pltpu.VMEM((blocks, Q), F32), pltpu.VMEM((mp - 1, blocks, Q), F32),
            pltpu.SemaphoreType.DMA((mp - 1,)), pltpu.SemaphoreType.DMA((mp - 1,)),
        ],
        compiler_params=params(collective_id=2, has_side_effects=True),
        cost_estimate=cost(2 * work, 8),
        name="carried",
    )(recv_a, recv_b, d_a, d_b, by_token, decay, cb, y, gate_values)
    return pl.pallas_call(
        norm_kernel,
        grid=(tokens // SHORT,),
        in_specs=[whole(blocks, Q), short(width), whole(1, width)],
        out_specs=short(width),
        out_shape=sds((tokens, width), BF),
        compiler_params=params(),
        cost_estimate=cost(2 * tokens * width, 4),
        name="normalise",
    )(squares, g, norm_gain[None])


def solution(mesh):
    in_specs = (
        P("seq", "mp"), P("seq", None), P("seq", "mp"), P("mp", "seq"), P("mp"),
        P(None, "mp"), P("mp"), P(), P(), P("mp"),
    )
    return jax.shard_map(
        on_device, mesh=mesh, in_specs=in_specs, out_specs=P("seq", "mp"), check_vma=False
    )
```

```python
import functools
import jax
import jax.numpy as jnp
from jax import lax
from jax.sharding import PartitionSpec as P
from jax.experimental import pallas as pl
from jax.experimental.pallas import tpu as pltpu

INNER = 16384
Q = 128
ROWS = 512
SHORT = 512
STATE = 128
HEAD = 64
LOG2E = 1.4426950408889634
F32 = jnp.float32
BF = jnp.bfloat16
HI = lax.Precision.HIGHEST
VMEM_LIMIT = 60 * 1024 * 1024


def iota(shape, dim):
    return lax.broadcasted_iota(jnp.int32, shape, dim)


def dot(a, b, **kw):
    return jnp.dot(a, b, preferred_element_type=F32, **kw)


def dot_rows(a, b, **kw):
    return lax.dot_general(a, b, (((1,), (1,)), ((), ())), preferred_element_type=F32, **kw)


def silu(v):
    return v * pl.reciprocal(1.0 + jnp.exp2(v * -LOG2E), approx=True)


def split3(v):
    hi = v.astype(BF).astype(F32)
    mid = (v - hi).astype(BF).astype(F32)
    return hi, mid, (v - hi) - mid


def over_channels(by_token, rs, h, first):
    return jnp.where(first, by_token[rs, h : h + 1], by_token[rs, h + 1 : h + 2])


def mix(tail, x, taps, bias):
    seen = jnp.concatenate([tail, x], axis=0)
    v = bias + taps[3:4] * x
    for back in (1, 2, 3):
        v = v + taps[3 - back : 4 - back] * pltpu.roll(seen, back, 0)[8:]
    return silu(v).astype(BF)


def prepare_kernel(raw, dlog, m_out, by_token, rows_out):
    heads, tokens = raw.shape
    blocks = tokens // Q
    r = jnp.concatenate([raw[:, c * Q : (c + 1) * Q] for c in range(blocks)], axis=0)
    step = jnp.maximum(r, 0.0) + jnp.log1p(jnp.exp(-jnp.abs(r)))
    same = iota((heads, heads), 0) == iota((heads, heads), 1)
    dlog_col = jnp.sum(jnp.where(same, dlog[...], 0.0), axis=1, keepdims=True)
    rate = jnp.broadcast_to(jnp.exp(dlog_col) * -LOG2E, (heads, Q))
    ld = jnp.concatenate([rate] * blocks, axis=0) * step
    upto = jnp.where(iota((Q, Q), 0) <= iota((Q, Q), 1), 1.0, 0.0)
    lc = dot(ld, upto, precision=HI)
    m = lc - jnp.log(step) * LOG2E
    to_end = jnp.exp2(lc[:, Q - 1 : Q] - m)
    decay = jnp.exp2(lc)
    ends = []
    for c in range(blocks):
        sl, rs = slice(c * Q, (c + 1) * Q), slice(c * heads, (c + 1) * heads)
        m_out[:, sl] = m[rs]
        parts = [lc[rs], to_end[rs], decay[rs], jnp.zeros((Q - 3 * heads, Q), F32)]
        turned = jnp.transpose(jnp.concatenate(parts, axis=0))
        by_token[sl] = turned
        ends.append(turned[Q - 1 : Q])
    ends = jnp.concatenate(ends, axis=0)
    lane = iota(ends.shape, 1)
    ends = jnp.where((lane >= 2 * heads) & (lane < 3 * heads), ends, 0.0)
    width = rows_out.shape[1]
    row, col = iota((Q, width), 0), iota((Q, width), 1)
    spread = jnp.where(row == (col >> 6) + 2 * heads, 1.0, 0.0).astype(BF)
    hi, mid, lo = (piece.astype(BF) for piece in split3(ends))
    rows_out[...] = dot(hi, spread) + dot(mid, spread) + dot(lo, spread)


def exchange(n, src, dst, send_sem, recv_sem):
    me = lax.axis_index("seq")

    def copy(d):
        return pltpu.make_async_remote_copy(
            src_ref=src, dst_ref=dst.at[d - 1], send_sem=send_sem.at[d - 1], recv_sem=recv_sem.at[d - 1],
            device_id={"seq": lax.rem(me + d, n)}, device_id_type=pl.DeviceIdType.MESH,
        )

    @pl.when(pl.program_id(0) == 0)
    def _():
        barrier = pltpu.get_barrier_semaphore()
        for d in range(1, n):
            pl.semaphore_signal(
                barrier, inc=1, device_id={"seq": lax.rem(me + d, n)}, device_id_type=pl.DeviceIdType.MESH
            )
        pl.semaphore_wait(barrier, n - 1)
        for d in range(1, n):
            pl.when(me + d < n)(lambda d=d: copy(d).start())

    def finish():
        @pl.when(pl.program_id(0) == pl.num_programs(0) - 1)
        def _():
            for d in range(1, n):
                pl.when(me + d < n)(lambda d=d: copy(d).wait_send())
                pl.when(me >= d)(lambda d=d: copy(d).wait_recv())

    return finish


def chunks(ref):
    return ref.shape[0] // Q


def rows_of(i):
    return pl.ds(pl.multiple_of(i * Q, Q), Q)


def states_body(first_head, heads, feat, by_token, decay, taps, off, ftail, input_map, x_out, d_out, e_out, ftl, acc, dec):
    c = pl.program_id(0)
    width = feat.shape[1]

    @pl.when(c == 0)
    def _():
        ftl[...] = ftail[...]
        acc[...] = jnp.zeros_like(acc)
        dec[...] = jnp.ones_like(dec)

    def one(i, carry):
        rs = rows_of(i)
        first = iota((Q, 128), 1) < HEAD
        row = decay[pl.ds(c * chunks(feat) + i, 1), :]
        bt = jnp.transpose(input_map(rs).astype(F32)).astype(BF)
        for j in range(width // 256):
            sl = slice(j * 256, (j + 1) * 256)
            xw = []
            for k in range(2):
                at = slice(j * 256 + k * 128, j * 256 + (k + 1) * 128)
                x = feat[rs, at].astype(F32)
                f = mix(ftl[:, at], x, taps[:, at], off[:, at])
                x_out[rs, at] = f
                ftl[:, at] = x[Q - 8 :]
                e = over_channels(by_token, rs, heads + first_head + 2 * (2 * j + k), first)
                xw.append((f.astype(F32) * e).astype(BF))
            d = dot(bt, jnp.concatenate(xw, axis=1))
            d_out[rs, sl] = d.astype(BF)
            acc[:, sl] = acc[:, sl] * row[:, sl] + d
        dec[...] = dec[...] * row
        return carry

    lax.fori_loop(0, chunks(feat), one, 0)

    @pl.when(c == pl.num_programs(0) - 1)
    def _():
        e_out[0:STATE] = acc[...].astype(BF)
        hi, mid, lo = split3(dec[...])
        which = iota(dec.shape, 0)
        rows = jnp.where(which == 0, hi, jnp.where(which == 1, mid, jnp.where(which == 2, lo, 0.0)))
        e_out[STATE : STATE + 16] = jnp.concatenate([rows, jnp.zeros_like(rows)], axis=0).astype(BF)


def states_a_kernel(
    heads, feat, by_token, decay, taps, off, ftail, coup, tapc, offc, ctail, x_out, d_out, e_out, cb_out, ftl, acc, dec, ctl
):
    @pl.when(pl.program_id(0) == 0)
    def _():
        ctl[...] = ctail[...]

    def input_map(rs):
        for j in (1, 0):
            sl = slice(j * STATE, (j + 1) * STATE)
            x = coup[rs, sl].astype(F32)
            f = mix(ctl[:, sl], x, tapc[:, sl], offc[:, sl])
            cb_out[rs, sl] = f
            ctl[:, sl] = x[Q - 8 :]
        return f

    states_body(0, heads, feat, by_token, decay, taps, off, ftail, input_map, x_out, d_out, e_out, ftl, acc, dec)


def states_b_kernel(
    heads, n, feat, by_token, decay, taps, off, ftail, cb, e_a, x_out, d_out, e_out, recv, ftl, acc, dec, send_sem, recv_sem
):
    finish = exchange(n, e_a, recv, send_sem, recv_sem)
    states_body(
        heads // 2, heads, feat, by_token, decay, taps, off, ftail, lambda rs: cb[rs, :STATE],
        x_out, d_out, e_out, ftl, acc, dec,
    )
    finish()


def inside_kernel(n, x_a, x_b, cb, m, lt, e_b, y_out, recv, send_sem, recv_sem):
    finish = exchange(n, e_b, recv, send_sem, recv_sem)
    causal = iota((Q, Q), 0) >= iota((Q, Q), 1)
    first = jnp.where(iota((Q, Q), 1) < HEAD, 1.0, 0.0)
    mask_a, mask_b = first.astype(BF), (1.0 - first).astype(BF)
    half = x_a.shape[1] // 128

    def one(i, carry):
        rs = rows_of(i)
        scores = dot_rows(cb[rs, STATE:], cb[rs, :STATE])
        for p in range(2 * half):
            ws = []
            for h in (2 * p, 2 * p + 1):
                decay = jnp.exp2(lt[rs, h : h + 1] - m[h : h + 1, rs])
                ws.append((jnp.where(causal, decay, 0.0) * scores).astype(BF))
            x = x_a if p < half else x_b
            xp = x[rs, (p % half) * 128 : (p % half + 1) * 128]
            both = jnp.concatenate([xp * mask_a, xp * mask_b], axis=0)
            y = dot(jnp.concatenate(ws, axis=1), both)
            y_out[rs, p * 128 : (p + 1) * 128] = y.astype(BF)
        return carry

    lax.fori_loop(0, chunks(x_a), one, 0)
    finish()


def carried_kernel(
    heads, others, n, recv_a, recv_b, d_a, d_b, by_token, decay, cb, y_in, gate,
    g_out, ss_out, state, ss, slots, send_sem, recv_sem,
):
    width = gate.shape[1]
    half = width // 2
    c = pl.program_id(0)
    section, me = lax.axis_index("seq"), lax.axis_index("mp")

    def copy(d):
        return pltpu.make_async_remote_copy(
            src_ref=ss, dst_ref=slots.at[d - 1], send_sem=send_sem.at[d - 1], recv_sem=recv_sem.at[d - 1],
            device_id={"mp": lax.rem(me + d, n)}, device_id_type=pl.DeviceIdType.MESH,
        )

    @pl.when(c == 0)
    def _():
        barrier = pltpu.get_barrier_semaphore()
        for d in range(1, n):
            pl.semaphore_signal(
                barrier, inc=1, device_id={"mp": lax.rem(me + d, n)}, device_id_type=pl.DeviceIdType.MESH
            )
        pl.semaphore_wait(barrier, n - 1)
        for j in range(width // 256):
            recv, at = (recv_a, j * 256) if j * 256 < half else (recv_b, j * 256 - half)
            total = jnp.zeros((STATE, 256), F32)
            through = jnp.ones((1, 256), F32)
            for d in range(others):
                came = section > d
                end = recv[d, :STATE, at : at + 256].astype(F32)
                rows = recv[d, STATE : STATE + 16, at : at + 256].astype(F32)
                total = total + jnp.where(came, through * end, 0.0)
                through = jnp.where(came, through * (rows[0:1] + rows[1:2] + rows[2:3]), 0.0)
            state[:, j * 256 : (j + 1) * 256] = total

    def one(i, carry):
        rs = rows_of(i)
        first = iota((Q, 128), 1) < HEAD
        out_map = cb[rs, STATE:]
        row = decay[pl.ds(c * chunks(gate) + i, 1), :]
        acc = jnp.zeros((Q, 128), F32)
        for j in range(width // 256):
            sl = slice(j * 256, (j + 1) * 256)
            d, at = (d_a, j * 256) if j * 256 < half else (d_b, j * 256 - half)
            s = state[:, sl]
            new = dot(out_map, s.astype(BF))
            state[:, sl] = s * row[:, sl] + d[rs, at : at + 256].astype(F32)
            for k in range(2):
                part = slice(j * 256 + k * 128, j * 256 + (k + 1) * 128)
                e = over_channels(by_token, rs, 2 * heads + 2 * (2 * j + k), first)
                y = y_in[rs, part].astype(F32) + new[:, k * 128 : (k + 1) * 128] * e
                g = y * silu(gate[rs, part].astype(F32))
                acc = acc + g * g
                g_out[rs, part] = g.astype(BF)
        squares = dot_rows(jnp.ones((8, Q), F32), acc, precision=HI)
        ss[pl.ds(c * chunks(gate) + i, 1), :] = squares[0:1]
        return carry

    lax.fori_loop(0, chunks(gate), one, 0)

    @pl.when(c == pl.num_programs(0) - 1)
    def _():
        for d in range(1, n):
            copy(d).start()
        total = ss[...]
        for d in range(1, n):
            copy(d).wait()
            total = total + slots[d - 1]
        ss_out[...] = total


def norm_kernel(ss, g, gain, out):
    c = pl.program_id(0)

    def one(i, carry):
        rs = rows_of(i)
        scale = lax.rsqrt(ss[pl.ds(c * chunks(g) + i, 1), :] * (1.0 / INNER) + 1e-5)
        scale = jnp.transpose(jnp.broadcast_to(scale, (Q, Q)))
        for j in range(g.shape[1] // 128):
            sl = slice(j * 128, (j + 1) * 128)
            out[rs, sl] = (g[rs, sl].astype(F32) * gain[:, sl] * scale).astype(BF)
        return carry

    lax.fori_loop(0, chunks(g), one, 0)


def passed_along(block, distance):
    devices = range(lax.axis_size("seq"))
    route = [(i - distance, i) for i in devices if i - distance in devices]
    return lax.ppermute(block, "seq", route)


def params(**kw):
    return pltpu.CompilerParams(vmem_limit_bytes=VMEM_LIMIT, **kw)


def on_device(
    features, coupling, gate_values, step_raw, decay_log,
    feature_taps, feature_offset, coupling_taps, coupling_offset, norm_gain,
):
    tokens, width = features.shape
    heads = decay_log.shape[0]
    blocks = tokens // Q
    grid = (tokens // ROWS,)
    half = width // 2
    seq, mp = lax.axis_size("seq"), lax.axis_size("mp")
    tail = feature_taps.shape[0] - 1
    ends = jnp.concatenate([features[tokens - tail :], coupling[tokens - tail :]], axis=1)
    prior = passed_along(ends, 1)
    prior = jnp.pad(prior, ((8 - tail, 0), (0, 0))).astype(F32)

    def whole(*shape):
        return pl.BlockSpec(shape, lambda c: (0,) * len(shape))

    def rows(n, at=0):
        return pl.BlockSpec((ROWS, n), lambda c: (c, at))

    def short(n):
        return pl.BlockSpec((SHORT, n), lambda c: (c, 0))

    def side(n, at):
        return pl.BlockSpec((n, half), lambda c: (0, at))

    hbm = pl.BlockSpec(memory_space=pl.ANY)
    vmem = pl.BlockSpec(memory_space=pltpu.VMEM)
    sds = jax.ShapeDtypeStruct
    work = 2 * tokens * width * STATE

    def cost(flops, moved):
        return pl.CostEstimate(flops=flops, bytes_accessed=moved * tokens * width, transcendentals=0)

    m, by_token, decay = pl.pallas_call(
        prepare_kernel,
        in_specs=[vmem, vmem],
        out_specs=[vmem] * 3,
        out_shape=[sds((heads, tokens), F32), sds((tokens, Q), F32), sds((blocks, width), F32)],
        compiler_params=params(),
        cost_estimate=pl.CostEstimate(flops=work // 64, bytes_accessed=tokens * 1024, transcendentals=0),
        name="prepare",
    )(step_raw, decay_log[None])

    part = sds((tokens, half), BF)
    end_shape = sds((STATE + 16, half), BF)
    recv_shape = sds((seq - 1, STATE + 16, half), BF)
    keep = [
        pltpu.VMEM((8, half), F32),
        pltpu.VMEM((STATE, half), F32), pltpu.VMEM((8, half), F32),
    ]
    sems = [pltpu.SemaphoreType.DMA((seq - 1,)), pltpu.SemaphoreType.DMA((seq - 1,))]

    def state_specs(at):
        return [rows(half, at), rows(Q), side(blocks, at), side(4, at), side(1, at), side(8, at)]

    state_args = (features, by_token, decay, feature_taps, feature_offset[None], prior)
    x_a, d_a, e_a, cb = pl.pallas_call(
        functools.partial(states_a_kernel, heads),
        grid=grid,
        in_specs=state_specs(0)
        + [rows(2 * STATE), whole(4, 2 * STATE), whole(1, 2 * STATE), pl.BlockSpec((8, 2 * STATE), lambda c: (0, width // (2 * STATE)))],
        out_specs=[rows(half), rows(half), whole(STATE + 16, half), rows(2 * STATE)],
        out_shape=[part, part, end_shape, sds((tokens, 2 * STATE), BF)],
        scratch_shapes=keep + [pltpu.VMEM((8, 2 * STATE), F32)],
        compiler_params=params(),
        cost_estimate=cost(work, 3),
        name="states_a",
    )(*state_args, coupling, coupling_taps, coupling_offset[None], prior)
    x_b, d_b, e_b, recv_a = pl.pallas_call(
        functools.partial(states_b_kernel, heads, seq),
        grid=grid,
        in_specs=state_specs(1) + [rows(2 * STATE), hbm],
        out_specs=[rows(half), rows(half), whole(STATE + 16, half), hbm],
        out_shape=[part, part, end_shape, recv_shape],
        scratch_shapes=keep + sems,
        compiler_params=params(collective_id=0, has_side_effects=True),
        cost_estimate=cost(work, 3),
        name="states_b",
    )(*state_args, cb, e_a)
    y, recv_b = pl.pallas_call(
        functools.partial(inside_kernel, seq),
        grid=grid,
        in_specs=[rows(half), rows(half), rows(2 * STATE), pl.BlockSpec((heads, ROWS), lambda c: (0, c)), rows(Q), hbm],
        out_specs=[rows(width), hbm],
        out_shape=[sds((tokens, width), BF), recv_shape],
        scratch_shapes=sems,
        compiler_params=params(collective_id=1, has_side_effects=True),
        cost_estimate=cost(4 * work, 4),
        name="inside",
    )(x_a, x_b, cb, m, by_token, e_b)
    g, squares = pl.pallas_call(
        functools.partial(carried_kernel, heads, seq - 1, mp),
        grid=(tokens // SHORT,),
        in_specs=[
            whole(seq - 1, STATE + 16, half), whole(seq - 1, STATE + 16, half),
            short(half), short(half), short(Q), whole(blocks, width), short(2 * STATE), short(width), short(width),
        ],
        out_specs=[short(width), whole(blocks, Q)],
        out_shape=[sds((tokens, width), BF), sds((blocks, Q), F32)],
        scratch_shapes=[
            pltpu.VMEM((STATE, width), F32), pltpu.VMEM((blocks, Q), F32), pltpu.VMEM((mp - 1, blocks, Q), F32),
            pltpu.SemaphoreType.DMA((mp - 1,)), pltpu.SemaphoreType.DMA((mp - 1,)),
        ],
        compiler_params=params(collective_id=2, has_side_effects=True),
        cost_estimate=cost(2 * work, 8),
        name="carried",
    )(recv_a, recv_b, d_a, d_b, by_token, decay, cb, y, gate_values)
    return pl.pallas_call(
        norm_kernel,
        grid=(tokens // SHORT,),
        in_specs=[whole(blocks, Q), short(width), whole(1, width)],
        out_specs=short(width),
        out_shape=sds((tokens, width), BF),
        compiler_params=params(),
        cost_estimate=cost(2 * tokens * width, 4),
        name="normalise",
    )(squares, g, norm_gain[None])


def solution(mesh):
    in_specs = (
        P("seq", "mp"), P("seq", None), P("seq", "mp"), P("mp", "seq"), P("mp"),
        P(None, "mp"), P("mp"), P(), P(), P("mp"),
    )
    return jax.shard_map(
        on_device, mesh=mesh, in_specs=in_specs, out_specs=P("seq", "mp"), check_vma=False
    )
```
